32 devices in a mesh: groups: 2 (over y), seq: 4 (over z), help: 2 (over x), head: 2 (over core).
Axes of the slice: x: 2, y: 2, z: 4, core: 2. Of those that a mesh axis runs over, the one named last changes fastest.
Arguments:
- query_rows: bfloat16 [2048, 2048], P(('groups', 'seq', 'help'), 'head'), parts along dimension 0, may hold values from -5.5 to 5.5
- key_rows: bfloat16 [2048, 2048], P(('groups', 'seq', 'help'), 'head'), parts along dimension 0, may hold values from -5.5 to 5.5
- value_rows: bfloat16 [2048, 2048], P(('groups', 'seq', 'help'), 'head'), parts along dimension 0, may hold values from -6 to 6
- out_grad: bfloat16 [2048, 2048], P(('groups', 'seq', 'help'), 'head'), parts along dimension 0, may hold values from -6 to 6
- cluster_ids: int32 [16, 2048, 1], P('head', ('groups', 'seq', 'help')), parts along dimension 1, may hold values from 0 to 127; in each aligned block of 128 rows (0 to 127, 128 to 255, ..., all dimensions but the last counted through in order) at most 2 rows name the same one
- cluster_slots: int32 [32, 128], P(('groups', 'head')), parts along dimension 0, may hold values from 0 to 127, each once within a row
Outputs:
- attended: bfloat16 [2048, 2048], P(('groups', 'seq', 'help'), 'head'), parts along dimension 0
- grad_queries: bfloat16 [2048, 2048], P(('groups', 'seq', 'help'), 'head'), parts along dimension 0
- grad_keys: bfloat16 [2048, 2048], P(('groups', 'seq', 'help'), 'head'), parts along dimension 0
- grad_values: bfloat16 [2048, 2048], P(('groups', 'seq', 'help'), 'head'), parts along dimension 0
- centroid_sums: float32 [32, 128, 128], P(('groups', 'head'), ('seq', 'help')), parts along dimension 0
The draws below stay inside these ranges and needn't reach their ends.
There are 2 independent parts, one for each index of `groups`. The reference program is written for one: setup_inputs(seed, part) draws one part's arguments, and reference() takes and returns one part's arrays. A program takes and returns all parts, laid end to end along the dimension named above; each array names one. Nothing has to cross between parts.
Inputs may be any that keep to these rules, and one draw needn't show every extreme that they name: `cluster_ids`: in each aligned block of 128 rows (one head's tokens on one device) no cluster is named more than 2 times, a bound that some block reaches. `cluster_slots`: each head's row names every slot once.
All inputs are finite; a program needn't handle non-finite values.
Results may differ from the reference program's by a relative error of at most 0.0062.
Values may be sent and summed in bfloat16 or wider, within the bound.
A program may use at most 64 MiB of HBM per device.

```python
import math
import jax
import jax.numpy as jnp
import numpy as np
from jax import lax

HEADS = 16
DH = 128
CLUSTERS = 128
BLK = 256
TOK_DEV = 128
MOST = 2
TOKENS = 1024
CAP = 16


def draw_query_rows(key, part):
    key = jax.random.fold_in(key, 11)
    base = jnp.clip(jax.random.normal(key, (TOKENS, HEADS * DH), jnp.float32), -5.5, 5.5)
    return base.astype(jnp.bfloat16)


def draw_key_rows(key, part):
    key = jax.random.fold_in(key, 12)
    base = jnp.clip(jax.random.normal(key, (TOKENS, HEADS * DH), jnp.float32), -5.5, 5.5)
    return base.astype(jnp.bfloat16)


def shard_levels(stream_key, dims, shards, smallest, high):
    gain = 1.0
    for position, shards_of in shards:
        draws = jax.random.uniform(jax.random.fold_in(jax.random.fold_in(stream_key, 6), position), (shards_of,), jnp.float32, smallest / len(shards), high / len(shards))
        gain = gain * jnp.repeat(jnp.exp(draws), dims[position] // shards_of).reshape((-1,) + (1,) * (len(dims) - 1 - position))
    return gain


def routed_block(key, own, number, rows, count, top, limit, lean):
    sequence = jax.random.permutation(key, count)
    heavy_load, ordinary = load_shares(count, rows * top, limit, lean, True), load_shares(count, rows * top, limit, lean, False)
    places = jnp.arange(count)

    def named(tallies, offset_by):
        used = int((tallies > 0).sum())
        fixed = max(1, used // 4)
        passed = fixed + (places - fixed + offset_by * (used - fixed)) % max(1, count - fixed)
        return jnp.zeros((count,), jnp.int32).at[sequence[jnp.where(places < fixed, places, passed)]].set(jnp.asarray(tallies, jnp.int32))

    tallies = jnp.where(number % 4 == 0, named(heavy_load, number // 4), named(ordinary, number - number // 4 - 1))
    mixed = jax.random.permutation(jax.random.fold_in(own, 3), count)
    donor, taker = mixed[0:count // 2 * 2:2], mixed[1:count // 2 * 2:2]
    room = jnp.minimum(tallies[donor] - 1, limit - tallies[taker]) // 2
    room = jnp.where((donor == sequence[0]) | (taker == sequence[0]) | (tallies[taker] == 0), 0, jnp.maximum(room, 0))
    passed = jax.random.randint(jax.random.fold_in(own, 4), (count // 2,), 0, 1 << 20) % (room + 1)
    tallies = tallies.at[donor].add(-passed).at[taker].add(passed)
    items = jnp.searchsorted(jnp.cumsum(tallies), jnp.arange(rows * top), side="right").astype(jnp.int32)
    table = items.reshape(top, rows).T
    table = table[jax.random.permutation(jax.random.fold_in(own, 1), rows)]
    offset_by = jax.random.randint(jax.random.fold_in(own, 2), (rows, 1), 0, top)
    return jnp.take_along_axis(table, (jnp.arange(top)[None, :] + offset_by) % top, axis=1)


def load_shares(number_of, total, bound, lean, full):
    portions = [(1 << 20) // math.isqrt(grade ** lean) + 1 for grade in range(1, number_of + 1)]
    largest = bound if full else min(bound, max(-(-total // number_of), total * portions[0] // sum(portions)))
    least = 1 if total - largest >= number_of - 1 else 0
    given, spare = [largest] + [least] * (number_of - 1), total - largest - least * (number_of - 1)
    while spare > 0:
        candidates = [i for i in range(1, number_of) if given[i] < largest] or [i for i in range(1, number_of) if given[i] < bound]
        whole, budget = sum([portions[i] for i in candidates]), spare
        for i in candidates:
            extra = min(bound - given[i], max(1, budget * portions[i] // whole), spare)
            given[i] = given[i] + extra
            spare = spare - extra
    return np.array(given)


def scatter_about(stream_key, shape, scale, bound, shards=(), kind=jnp.bfloat16):
    values = scale * jax.random.normal(stream_key, shape, jnp.float32)
    if shards:
        values = values * shard_levels(stream_key, shape, shards, -0.22, 0.18)
    return jnp.clip(values, -bound, bound).astype(kind)


def setup_inputs(seed: int = 0, part: int = 0) -> dict:
    key_of = jax.random.split(jax.random.key(seed), 7)
    part_splits = jax.random.split(jax.random.fold_in(key_of[6], part), 7)
    query_rows = draw_query_rows(jax.random.fold_in(jax.random.fold_in(key_of[6], part), 71), part)
    key_rows = draw_key_rows(jax.random.fold_in(jax.random.fold_in(key_of[6], part), 71), part)
    value_rows = scatter_about(part_splits[2], (TOKENS, HEADS * DH), 1.0, 6.0, ((0, 8), (1, 2)))
    out_grad = scatter_about(part_splits[3], (TOKENS, HEADS * DH), 1.0, 6.0, ((0, 8), (1, 2)))
    cluster_ids_keys = jax.random.split(jax.random.fold_in(part_splits[4], 1), HEADS * TOKENS // TOK_DEV)
    cluster_ids_turns = jax.random.permutation(jax.random.fold_in(part_splits[4], 3), HEADS * TOKENS // TOK_DEV)
    cluster_ids = jax.vmap(lambda own, number: routed_block(jax.random.fold_in(part_splits[4], 2), own, number, TOK_DEV, CLUSTERS, 1, MOST, 2))(cluster_ids_keys, cluster_ids_turns).reshape((HEADS, TOKENS, 1))
    cluster_slots = jax.vmap(lambda own: jax.random.permutation(own, CLUSTERS))(jax.random.split(part_splits[5], HEADS)).reshape((HEADS, CLUSTERS)).astype(jnp.int32)
    return dict(query_rows=query_rows, key_rows=key_rows, value_rows=value_rows, out_grad=out_grad, cluster_ids=cluster_ids, cluster_slots=cluster_slots)


def unit_keys(key_part):
    key_float = key_part.astype(jnp.float32)
    spread = lax.optimization_barrier(jnp.mean(key_float * key_float, axis=-1, keepdims=True))
    return key_float * lax.rsqrt(spread + 1e-06) * key_part.shape[-1] ** (-0.5)

def centroid_sum(packed_rows, token_pos):
    depth = packed_rows.shape[-1] // 4
    units = unit_keys(packed_rows[:, depth:2 * depth])
    return lax.optimization_barrier(jnp.sum(jnp.where(token_pos[:, None] >= 0, units, 0.0), axis=0))

def cluster_attention(packed_rows, token_pos):
    depth = packed_rows.shape[-1] // 4
    count = packed_rows.shape[0]
    query_part = packed_rows[:, :depth]
    key_part = packed_rows[:, depth:2 * depth]
    value_part = packed_rows[:, 2 * depth:3 * depth]
    grad_part = packed_rows[:, 3 * depth:]
    valid = token_pos >= 0
    rank = jnp.cumsum(valid.astype(jnp.int32)) - 1
    block_id = rank // BLK
    allowed = valid[:, None] & valid[None, :] & (block_id[:, None] == block_id[None, :])
    allowed = allowed & (token_pos[None, :] <= token_pos[:, None])
    allowed = allowed | jnp.eye(count, dtype=bool)
    scale = depth ** (-0.5)
    scores = lax.dot_general(query_part, key_part, (((1,), (1,)), ((), ())), preferred_element_type=jnp.float32) * scale
    scores = jnp.where(allowed, scores, -1e+30)
    peak = lax.optimization_barrier(jnp.max(scores, axis=1, keepdims=True))
    weights = jnp.exp(scores - peak)
    weights = weights / lax.optimization_barrier(jnp.sum(weights, axis=1, keepdims=True))
    weights_low = weights.astype(jnp.bfloat16)
    context = jnp.dot(weights_low, value_part, preferred_element_type=jnp.float32)
    grad_value = lax.dot_general(weights_low, grad_part, (((0,), (0,)), ((), ())), preferred_element_type=jnp.float32)
    grad_weights = lax.dot_general(grad_part, value_part, (((1,), (1,)), ((), ())), preferred_element_type=jnp.float32)
    delta = lax.optimization_barrier(jnp.sum(grad_part.astype(jnp.float32) * context, axis=1, keepdims=True))
    grad_scores = (weights * (grad_weights - delta)).astype(jnp.bfloat16)
    grad_query = jnp.dot(grad_scores, key_part, preferred_element_type=jnp.float32) * scale
    grad_key = lax.dot_general(grad_scores, query_part, (((0,), (0,)), ((), ())), preferred_element_type=jnp.float32) * scale
    return jnp.concatenate([context, grad_query, grad_key, grad_value], axis=1).astype(jnp.bfloat16)

def reference(query_rows, key_rows, value_rows, out_grad, cluster_ids, cluster_slots):
    packed = jnp.concatenate([part.reshape(TOKENS, HEADS, DH) for part in (query_rows, key_rows, value_rows, out_grad)], axis=2)
    packed = packed.transpose(1, 0, 2)

    def per_head(head_item):
        head_rows, labels, slots = head_item
        order = jnp.argsort(labels, stable=True).astype(jnp.int32)
        counts = lax.optimization_barrier(jnp.sum((labels[:, None] == jnp.arange(CLUSTERS, dtype=jnp.int32)[None, :]).astype(jnp.int32), axis=0)).astype(jnp.int32)
        starts = (jnp.cumsum(counts) - counts).astype(jnp.int32)
        sorted_rows = jnp.concatenate([head_rows[order], jnp.zeros((CAP, 4 * DH), jnp.bfloat16)], axis=0)
        sorted_pos = jnp.concatenate([order, jnp.full((CAP,), -1, jnp.int32)], axis=0)

        def per_cluster(carry, cluster):
            out_acc, sums = carry
            start = starts[cluster].astype(jnp.int32)
            block_rows = lax.dynamic_slice_in_dim(sorted_rows, start, CAP, 0)
            block_pos = lax.dynamic_slice_in_dim(sorted_pos, start, CAP, 0)
            block_pos = jnp.where(jnp.arange(CAP, dtype=jnp.int32) < counts[cluster], block_pos, -1).astype(jnp.int32)
            result = cluster_attention(block_rows, block_pos)
            target = jnp.where(block_pos >= 0, block_pos, TOKENS).astype(jnp.int32)
            out_acc = out_acc.at[target].set(result, mode='drop')
            sums = sums.at[slots[cluster]].set(centroid_sum(block_rows, block_pos))
            return ((out_acc, sums), None)
        start_carry = (jnp.zeros((TOKENS, 4 * DH), jnp.bfloat16), jnp.zeros((CLUSTERS, DH), jnp.float32))
        (out_acc, sums), _ = lax.scan(per_cluster, start_carry, jnp.arange(CLUSTERS, dtype=jnp.int32))
        return (out_acc, sums)
    results, centroid_sums = lax.map(per_head, (packed, cluster_ids[:, :, 0], cluster_slots))
    results = results.transpose(1, 0, 2)
    pieces = [results[:, :, index * DH:(index + 1) * DH].reshape(TOKENS, HEADS * DH) for index in range(4)]
    return (pieces[0], pieces[1], pieces[2], pieces[3], centroid_sums)
```

```python
import functools

import jax
import jax.numpy as jnp
from jax import lax
from jax.experimental import pallas as pl
from jax.experimental.pallas import tpu as pltpu
from jax.sharding import PartitionSpec as P

BLK = 256
MOST = 2


def unit_keys(key_part):
    key_float = key_part.astype(jnp.float32)
    spread = jnp.mean(key_float * key_float, axis=-1, keepdims=True)
    return key_float * lax.rsqrt(spread + 1e-06) * key_part.shape[-1] ** (-0.5)


def cluster_attention(packed_rows, token_pos):
    depth = packed_rows.shape[-1] // 4
    count = packed_rows.shape[0]
    query_part = packed_rows[:, :depth]
    key_part = packed_rows[:, depth : 2 * depth]
    value_part = packed_rows[:, 2 * depth : 3 * depth]
    grad_part = packed_rows[:, 3 * depth :]
    valid = token_pos >= 0
    rank = jnp.cumsum(valid.astype(jnp.int32)) - 1
    block_id = rank // BLK
    allowed = valid[:, None] & valid[None, :] & (block_id[:, None] == block_id[None, :])
    allowed = allowed & (token_pos[None, :] <= token_pos[:, None])
    allowed = allowed | jnp.eye(count, dtype=bool)
    scale = depth ** (-0.5)
    scores = (
        lax.dot_general(
            query_part, key_part, (((1,), (1,)), ((), ())), preferred_element_type=jnp.float32
        )
        * scale
    )
    scores = jnp.where(allowed, scores, -1e30)
    peak = jnp.max(scores, axis=1, keepdims=True)
    weights = jnp.exp(scores - peak)
    weights = weights / jnp.sum(weights, axis=1, keepdims=True)
    weights_low = weights.astype(jnp.bfloat16)
    context = jnp.dot(weights_low, value_part, preferred_element_type=jnp.float32)
    grad_value = lax.dot_general(
        weights_low, grad_part, (((0,), (0,)), ((), ())), preferred_element_type=jnp.float32
    )
    grad_weights = lax.dot_general(
        grad_part, value_part, (((1,), (1,)), ((), ())), preferred_element_type=jnp.float32
    )
    delta = jnp.sum(grad_part.astype(jnp.float32) * context, axis=1, keepdims=True)
    grad_scores = (weights * (grad_weights - delta)).astype(jnp.bfloat16)
    grad_query = jnp.dot(grad_scores, key_part, preferred_element_type=jnp.float32) * scale
    grad_key = (
        lax.dot_general(
            grad_scores, query_part, (((0,), (0,)), ((), ())), preferred_element_type=jnp.float32
        )
        * scale
    )
    return jnp.concatenate([context, grad_query, grad_key, grad_value], axis=1).astype(jnp.bfloat16)


def owner_work(arrived, arrived_pos):
    head_count, per_device, source_count, most_count, packed_width = arrived.shape
    flat_rows = arrived.reshape(head_count, per_device, source_count * most_count, packed_width)
    flat_pos = arrived_pos.reshape(head_count, per_device, source_count * most_count)

    def one_head(head_pair):
        return jax.vmap(cluster_attention)(head_pair[0], head_pair[1])

    results = lax.map(one_head, (flat_rows, flat_pos)).reshape(arrived.shape)
    owner_sums = jnp.zeros((head_count, 1), jnp.float32)
    return (results, owner_sums)


def local(query_rows, key_rows, value_rows, out_grad, cluster_ids, cluster_slots):
    token_count, width = query_rows.shape
    local_heads, cluster_total = cluster_slots.shape
    depth = width // local_heads
    seq_size = lax.axis_size("seq")
    help_size = lax.axis_size("help")
    device_count = seq_size * help_size
    per_device = cluster_total // device_count
    packed = jnp.concatenate(
        [
            piece.reshape(token_count, local_heads, depth)
            for piece in (query_rows, key_rows, value_rows, out_grad)
        ],
        axis=2,
    )
    packed = packed.transpose(1, 0, 2)
    labels = cluster_ids[:, :, 0]
    matches = labels[:, :, None] == jnp.arange(cluster_total, dtype=jnp.int32)[None, None, :]
    slot_of = jnp.sum(jnp.where(matches, cluster_slots[:, None, :], 0), axis=2)
    positions = jnp.arange(token_count, dtype=jnp.int32)
    earlier = (labels[:, :, None] == labels[:, None, :]) & (
        positions[None, None, :] < positions[None, :, None]
    )
    within = jnp.sum(earlier.astype(jnp.int32), axis=2)
    target = slot_of // per_device
    column = slot_of % per_device
    flat_slot = (column * device_count + target) * MOST + within
    slot_total = per_device * device_count * MOST
    head_index = jnp.arange(local_heads, dtype=jnp.int32)[:, None]
    send_rows = (
        jnp.zeros((local_heads, slot_total, 4 * depth), jnp.bfloat16)
        .at[head_index, flat_slot]
        .set(packed)
    )
    global_pos = lax.axis_index(("seq", "help")) * token_count + positions
    send_pos = (
        jnp.full((local_heads, slot_total), -1, jnp.int32)
        .at[head_index, flat_slot]
        .set(jnp.broadcast_to(global_pos, (local_heads, token_count)))
    )
    grid_rows = (local_heads, per_device, device_count, MOST, 4 * depth)
    results, owner_sums = owner_work(
        lax.all_to_all(
            send_rows.reshape(grid_rows), ("seq", "help"), split_axis=2, concat_axis=2, tiled=True
        ),
        lax.all_to_all(
            send_pos.reshape(grid_rows[:-1]),
            ("seq", "help"),
            split_axis=2,
            concat_axis=2,
            tiled=True,
        ),
    )
    returned, owner_sums = (
        lax.all_to_all(results, ("seq", "help"), split_axis=2, concat_axis=2, tiled=True),
        owner_sums,
    )
    gathered = returned.reshape(local_heads, slot_total, 4 * depth)[head_index, flat_slot]
    gathered = gathered.transpose(1, 0, 2)
    pieces = [
        gathered[:, :, index * depth : (index + 1) * depth].reshape(token_count, width)
        for index in range(4)
    ]
    units = unit_keys(packed[:, :, depth : 2 * depth])
    chosen = (
        slot_of[:, :, None]
        == jnp.arange(lax.axis_size(("seq", "help")) * per_device, dtype=jnp.int32)[None, None, :]
    )
    centroid_sums = lax.psum_scatter(
        jnp.einsum(
            "htc,htd->chd", chosen.astype(jnp.float32), units, precision=lax.Precision.HIGHEST
        ),
        ("seq", "help"),
        scatter_dimension=0,
        tiled=True,
    ).transpose(1, 0, 2)
    return (pieces[0], pieces[1], pieces[2], pieces[3], centroid_sums)


MASKED = -1e30


def head_kernel(
    seq_size,
    help_size,
    q_ref,
    k_ref,
    v_ref,
    g_ref,
    ids_ref,
    slots_ref,
    att_ref,
    dq_ref,
    dk_ref,
    dv_ref,
    sums_ref,
    q_all,
    k_all,
    v_all,
    g_all,
    ids_all,
    att_stage,
    dq_stage,
    dk_stage,
    dv_stage,
    sums_stage,
    dk_total,
    dv_total,
    send_in,
    recv_in,
    send_out,
    recv_out,
):
    devices = seq_size * help_size
    tokens = q_ref.shape[0]
    depth = q_all.shape[1]
    clusters = slots_ref.shape[2]
    owned = clusters // devices
    me = lax.axis_index("seq") * help_size + lax.axis_index("help")

    def place(index):
        return {"seq": index // help_size, "help": lax.rem(index, help_size)}

    def partner(step):
        return lax.rem(me + step, devices)

    def columns(index):
        return pl.ds(pl.multiple_of(index * depth, depth), depth)

    def rows(index):
        return pl.ds(pl.multiple_of(index * tokens, tokens), tokens)

    barrier = pltpu.get_barrier_semaphore()
    for step in range(1, devices):
        pl.semaphore_signal(
            barrier, inc=1, device_id=place(partner(step)), device_id_type=pl.DeviceIdType.MESH
        )

    sources = (k_ref, q_ref, v_ref, g_ref)
    landings = (k_all, q_all, v_all, g_all)

    own_in = [
        pltpu.make_async_copy(source.at[:, columns(me)], landing.at[rows(me)], send_in.at[0, item])
        for item, (source, landing) in enumerate(zip(sources, landings))
    ]
    own_in.append(pltpu.make_async_copy(ids_ref.at[me], ids_all.at[me], send_in.at[0, 4]))
    for copy in own_in:
        copy.start()
    pl.semaphore_wait(barrier, devices - 1)

    def inbound(step):
        target = partner(step)
        copies = [
            pltpu.make_async_remote_copy(
                src_ref=ids_ref.at[target],
                dst_ref=ids_all.at[me],
                send_sem=send_in.at[step, 4],
                recv_sem=recv_in.at[step, 4],
                device_id=place(target),
                device_id_type=pl.DeviceIdType.MESH,
            )
        ]
        for item, (source, landing) in enumerate(zip(sources, landings)):
            copies.append(
                pltpu.make_async_remote_copy(
                    src_ref=source.at[:, columns(target)],
                    dst_ref=landing.at[rows(me)],
                    send_sem=send_in.at[step, item],
                    recv_sem=recv_in.at[step, item],
                    device_id=place(target),
                    device_id_type=pl.DeviceIdType.MESH,
                )
            )
        return copies

    incoming = [inbound(step) for step in range(1, devices)]
    for copies in incoming:
        for copy in copies:
            copy.start()
    for copy in own_in:
        copy.wait()
    for copies in incoming:
        for copy in copies:
            copy.wait()

    stages = (att_stage, dq_stage, dk_stage, dv_stage)
    results = (att_ref, dq_ref, dk_ref, dv_ref)

    def outbound(target):
        return [
            pltpu.make_async_remote_copy(
                src_ref=stage.at[rows(target)],
                dst_ref=result.at[:, columns(me)],
                send_sem=send_out.at[target, item],
                recv_sem=recv_out.at[me, item],
                device_id=place(target),
                device_id_type=pl.DeviceIdType.MESH,
            )
            for item, (stage, result) in enumerate(zip(stages, results))
        ]

    def own_out(target):
        return [
            pltpu.make_async_copy(
                stage.at[rows(target)], result.at[:, columns(target)], send_out.at[target, item]
            )
            for item, (stage, result) in enumerate(zip(stages, results))
        ]

    labels = [ids_all[index].astype(jnp.float32) for index in range(devices)]
    label_row = jnp.concatenate(labels, axis=1)
    label_columns = [
        jnp.transpose(jnp.broadcast_to(label, (tokens, tokens)))[:, :1] for label in labels
    ]

    scale = depth ** (-0.5)
    group = 2 if devices % 2 == 0 else 1
    block = group * tokens
    blocks = devices // group
    dk_total[...] = jnp.zeros_like(dk_total)
    dv_total[...] = jnp.zeros_like(dv_total)
    earlier = lax.broadcasted_iota(jnp.int32, (block, block), 1) <= lax.broadcasted_iota(
        jnp.int32, (block, block), 0
    )
    for index in reversed(range(blocks)):
        low, high = index * block, (index + 1) * block
        query, grad = q_all[low:high], g_all[low:high]
        keys, values = k_all[:high], v_all[:high]
        label_column = jnp.concatenate(
            label_columns[index * group : (index + 1) * group], axis=0
        )
        allowed = label_column == label_row[:, :high]
        near = allowed[:, low:] & earlier
        allowed = near if low == 0 else jnp.concatenate([allowed[:, :low], near], axis=1)
        scores = (
            lax.dot_general(
                query, keys, (((1,), (1,)), ((), ())), preferred_element_type=jnp.float32
            )
            * scale
        )
        scores = jnp.where(allowed, scores, MASKED)
        peak = jnp.max(scores, axis=1, keepdims=True)
        weights = jnp.exp(scores - peak)
        weights = weights * (1.0 / jnp.sum(weights, axis=1, keepdims=True))
        weights_low = weights.astype(jnp.bfloat16)
        context = jnp.dot(weights_low, values, preferred_element_type=jnp.float32)
        dv_total[:high] += lax.dot_general(
            weights_low, grad, (((0,), (0,)), ((), ())), preferred_element_type=jnp.float32
        )
        grad_weights = lax.dot_general(
            grad, values, (((1,), (1,)), ((), ())), preferred_element_type=jnp.float32
        )
        delta = jnp.sum(grad.astype(jnp.float32) * context, axis=1, keepdims=True)
        grad_scores = (weights * (grad_weights - delta)).astype(jnp.bfloat16)
        att_stage[low:high] = context.astype(jnp.bfloat16)
        dq_stage[low:high] = (
            jnp.dot(grad_scores, keys, preferred_element_type=jnp.float32) * scale
        ).astype(jnp.bfloat16)
        dk_total[:high] += lax.dot_general(
            grad_scores, query, (((0,), (0,)), ((), ())), preferred_element_type=jnp.float32
        )
        dk_stage[low:high] = (dk_total[low:high] * scale).astype(jnp.bfloat16)
        dv_stage[low:high] = dv_total[low:high].astype(jnp.bfloat16)
        for target in range(index * group, (index + 1) * group):

            @pl.when(me != target)
            def _():
                for copy in outbound(target):
                    copy.start()

            @pl.when(me == target)
            def _():
                for copy in own_out(target):
                    copy.start()

    key_float = k_all[...].astype(jnp.float32)
    spread = jnp.mean(key_float * key_float, axis=1, keepdims=True)
    units = key_float * (lax.rsqrt(spread + 1e-06) * scale)
    units_high = units.astype(jnp.bfloat16)
    units_rest = (units - units_high.astype(jnp.float32)).astype(jnp.bfloat16)
    numbers = lax.broadcasted_iota(jnp.int32, (clusters, 1), 0)
    named = (numbers.astype(jnp.float32) == label_row).astype(jnp.bfloat16)
    owner_of = (numbers == slots_ref[me]).astype(jnp.bfloat16)
    chosen = jnp.dot(owner_of, named, preferred_element_type=jnp.float32).astype(jnp.bfloat16)
    sums_stage[...] = jnp.dot(
        chosen, units_high, preferred_element_type=jnp.float32
    ) + jnp.dot(chosen, units_rest, preferred_element_type=jnp.float32)

    def slots_at(target):
        return pl.ds(pl.multiple_of(target * owned, owned), owned)

    def sums_out(step):
        target = partner(step)
        return pltpu.make_async_remote_copy(
            src_ref=sums_stage.at[slots_at(target)],
            dst_ref=sums_ref.at[me],
            send_sem=send_in.at[step, 5],
            recv_sem=recv_in.at[step, 5],
            device_id=place(target),
            device_id_type=pl.DeviceIdType.MESH,
        )

    sums_copies = [sums_out(step) for step in range(1, devices)]
    sums_copies.append(
        pltpu.make_async_copy(sums_stage.at[slots_at(me)], sums_ref.at[me], send_in.at[0, 5])
    )
    for copy in sums_copies:
        copy.start()

    for target in range(devices):

        @pl.when(me != target)
        def _():
            for item, (stage, result) in enumerate(zip(stages, results)):
                copy = pltpu.make_async_remote_copy(
                    src_ref=stage.at[rows(target)],
                    dst_ref=result.at[:, columns(target)],
                    send_sem=send_out.at[target, item],
                    recv_sem=recv_out.at[target, item],
                    device_id=place(target),
                    device_id_type=pl.DeviceIdType.MESH,
                )
                copy.wait_send()
                copy.wait_recv()

        @pl.when(me == target)
        def _():
            for copy in own_out(target):
                copy.wait()

    for copy in sums_copies:
        copy.wait()


def routed_by_head(query_rows, key_rows, value_rows, out_grad, cluster_ids, cluster_slots):
    token_count, width = query_rows.shape
    local_heads, cluster_total = cluster_slots.shape
    depth = width // local_heads
    seq_size, help_size = lax.axis_size("seq"), lax.axis_size("help")
    devices = seq_size * help_size
    if devices != local_heads:
        return local(query_rows, key_rows, value_rows, out_grad, cluster_ids, cluster_slots)
    total = devices * token_count
    low = jnp.bfloat16
    full = (total, depth)
    return pl.pallas_call(
        functools.partial(head_kernel, seq_size, help_size),
        out_shape=[jax.ShapeDtypeStruct((token_count, width), low)] * 4
        + [jax.ShapeDtypeStruct((local_heads, cluster_total // devices, depth), jnp.float32)],
        in_specs=[pl.BlockSpec(memory_space=pl.ANY)] * 4
        + [pl.BlockSpec(memory_space=pltpu.VMEM)] * 2,
        out_specs=[pl.BlockSpec(memory_space=pl.ANY)] * 5,
        scratch_shapes=[pltpu.VMEM(full, low)] * 4
        + [pltpu.VMEM((devices, 1, token_count), jnp.int32)]
        + [pltpu.VMEM(full, low)] * 4
        + [pltpu.VMEM((cluster_total, depth), jnp.float32)]
        + [pltpu.VMEM(full, jnp.float32)] * 2
        + [pltpu.SemaphoreType.DMA((devices, 6))] * 2
        + [pltpu.SemaphoreType.DMA((devices, 4))] * 2,
        compiler_params=pltpu.CompilerParams(
            collective_id=0, has_side_effects=True, vmem_limit_bytes=48 * 1024 * 1024
        ),
    )(
        query_rows,
        key_rows,
        value_rows,
        out_grad,
        cluster_ids.reshape(local_heads, 1, token_count),
        cluster_slots.reshape(local_heads, 1, cluster_total),
    )


def solution(mesh):
    in_specs = (
        P(("groups", "seq", "help"), "head"),
        P(("groups", "seq", "help"), "head"),
        P(("groups", "seq", "help"), "head"),
        P(("groups", "seq", "help"), "head"),
        P("head", ("groups", "seq", "help"), None),
        P(("groups", "head"), None),
    )
    out_specs = (
        P(("groups", "seq", "help"), "head"),
        P(("groups", "seq", "help"), "head"),
        P(("groups", "seq", "help"), "head"),
        P(("groups", "seq", "help"), "head"),
        P(("groups", "head"), ("seq", "help"), None),
    )
    return jax.shard_map(routed_by_head, mesh=mesh, in_specs=in_specs, out_specs=out_specs, check_vma=False)
```

```python
import functools

import jax
import jax.numpy as jnp
from jax import lax
from jax.experimental import pallas as pl
from jax.experimental.pallas import tpu as pltpu
from jax.sharding import PartitionSpec as P

BLK = 256
MOST = 2


def unit_keys(key_part):
    key_float = key_part.astype(jnp.float32)
    spread = jnp.mean(key_float * key_float, axis=-1, keepdims=True)
    return key_float * lax.rsqrt(spread + 1e-06) * key_part.shape[-1] ** (-0.5)


def cluster_attention(packed_rows, token_pos):
    depth = packed_rows.shape[-1] // 4
    count = packed_rows.shape[0]
    query_part = packed_rows[:, :depth]
    key_part = packed_rows[:, depth : 2 * depth]
    value_part = packed_rows[:, 2 * depth : 3 * depth]
    grad_part = packed_rows[:, 3 * depth :]
    valid = token_pos >= 0
    rank = jnp.cumsum(valid.astype(jnp.int32)) - 1
    block_id = rank // BLK
    allowed = valid[:, None] & valid[None, :] & (block_id[:, None] == block_id[None, :])
    allowed = allowed & (token_pos[None, :] <= token_pos[:, None])
    allowed = allowed | jnp.eye(count, dtype=bool)
    scale = depth ** (-0.5)
    scores = (
        lax.dot_general(
            query_part, key_part, (((1,), (1,)), ((), ())), preferred_element_type=jnp.float32
        )
        * scale
    )
    scores = jnp.where(allowed, scores, -1e30)
    peak = jnp.max(scores, axis=1, keepdims=True)
    weights = jnp.exp(scores - peak)
    weights = weights / jnp.sum(weights, axis=1, keepdims=True)
    weights_low = weights.astype(jnp.bfloat16)
    context = jnp.dot(weights_low, value_part, preferred_element_type=jnp.float32)
    grad_value = lax.dot_general(
        weights_low, grad_part, (((0,), (0,)), ((), ())), preferred_element_type=jnp.float32
    )
    grad_weights = lax.dot_general(
        grad_part, value_part, (((1,), (1,)), ((), ())), preferred_element_type=jnp.float32
    )
    delta = jnp.sum(grad_part.astype(jnp.float32) * context, axis=1, keepdims=True)
    grad_scores = (weights * (grad_weights - delta)).astype(jnp.bfloat16)
    grad_query = jnp.dot(grad_scores, key_part, preferred_element_type=jnp.float32) * scale
    grad_key = (
        lax.dot_general(
            grad_scores, query_part, (((0,), (0,)), ((), ())), preferred_element_type=jnp.float32
        )
        * scale
    )
    return jnp.concatenate([context, grad_query, grad_key, grad_value], axis=1).astype(jnp.bfloat16)


def owner_work(arrived, arrived_pos):
    head_count, per_device, source_count, most_count, packed_width = arrived.shape
    flat_rows = arrived.reshape(head_count, per_device, source_count * most_count, packed_width)
    flat_pos = arrived_pos.reshape(head_count, per_device, source_count * most_count)

    def one_head(head_pair):
        return jax.vmap(cluster_attention)(head_pair[0], head_pair[1])

    results = lax.map(one_head, (flat_rows, flat_pos)).reshape(arrived.shape)
    owner_sums = jnp.zeros((head_count, 1), jnp.float32)
    return (results, owner_sums)


def local(query_rows, key_rows, value_rows, out_grad, cluster_ids, cluster_slots):
    token_count, width = query_rows.shape
    local_heads, cluster_total = cluster_slots.shape
    depth = width // local_heads
    seq_size = lax.axis_size("seq")
    help_size = lax.axis_size("help")
    device_count = seq_size * help_size
    per_device = cluster_total // device_count
    packed = jnp.concatenate(
        [
            piece.reshape(token_count, local_heads, depth)
            for piece in (query_rows, key_rows, value_rows, out_grad)
        ],
        axis=2,
    )
    packed = packed.transpose(1, 0, 2)
    labels = cluster_ids[:, :, 0]
    matches = labels[:, :, None] == jnp.arange(cluster_total, dtype=jnp.int32)[None, None, :]
    slot_of = jnp.sum(jnp.where(matches, cluster_slots[:, None, :], 0), axis=2)
    positions = jnp.arange(token_count, dtype=jnp.int32)
    earlier = (labels[:, :, None] == labels[:, None, :]) & (
        positions[None, None, :] < positions[None, :, None]
    )
    within = jnp.sum(earlier.astype(jnp.int32), axis=2)
    target = slot_of // per_device
    column = slot_of % per_device
    flat_slot = (column * device_count + target) * MOST + within
    slot_total = per_device * device_count * MOST
    head_index = jnp.arange(local_heads, dtype=jnp.int32)[:, None]
    send_rows = (
        jnp.zeros((local_heads, slot_total, 4 * depth), jnp.bfloat16)
        .at[head_index, flat_slot]
        .set(packed)
    )
    global_pos = lax.axis_index(("seq", "help")) * token_count + positions
    send_pos = (
        jnp.full((local_heads, slot_total), -1, jnp.int32)
        .at[head_index, flat_slot]
        .set(jnp.broadcast_to(global_pos, (local_heads, token_count)))
    )
    grid_rows = (local_heads, per_device, device_count, MOST, 4 * depth)
    results, owner_sums = owner_work(
        lax.all_to_all(
            send_rows.reshape(grid_rows), ("seq", "help"), split_axis=2, concat_axis=2, tiled=True
        ),
        lax.all_to_all(
            send_pos.reshape(grid_rows[:-1]),
            ("seq", "help"),
            split_axis=2,
            concat_axis=2,
            tiled=True,
        ),
    )
    returned, owner_sums = (
        lax.all_to_all(results, ("seq", "help"), split_axis=2, concat_axis=2, tiled=True),
        owner_sums,
    )
    gathered = returned.reshape(local_heads, slot_total, 4 * depth)[head_index, flat_slot]
    gathered = gathered.transpose(1, 0, 2)
    pieces = [
        gathered[:, :, index * depth : (index + 1) * depth].reshape(token_count, width)
        for index in range(4)
    ]
    units = unit_keys(packed[:, :, depth : 2 * depth])
    chosen = (
        slot_of[:, :, None]
        == jnp.arange(lax.axis_size(("seq", "help")) * per_device, dtype=jnp.int32)[None, None, :]
    )
    centroid_sums = lax.psum_scatter(
        jnp.einsum(
            "htc,htd->chd", chosen.astype(jnp.float32), units, precision=lax.Precision.HIGHEST
        ),
        ("seq", "help"),
        scatter_dimension=0,
        tiled=True,
    ).transpose(1, 0, 2)
    return (pieces[0], pieces[1], pieces[2], pieces[3], centroid_sums)


MASKED = -1e30


def head_kernel(
    seq_size,
    help_size,
    parts,
    q_ref,
    k_ref,
    v_ref,
    g_ref,
    ids_ref,
    slots_ref,
    att_ref,
    dq_ref,
    dk_ref,
    dv_ref,
    dk_far_ref,
    dv_far_ref,
    sums_ref,
    q_all,
    k_all,
    v_all,
    g_all,
    ids_all,
    att_stage,
    dq_stage,
    dk_stage,
    dv_stage,
    sums_stage,
    dk_total,
    dv_total,
    send_in,
    recv_in,
    send_ids,
    recv_ids,
    send_out,
    recv_out,
    send_sums,
    recv_sums,
):
    devices = seq_size * help_size
    owners = devices // parts
    share, _, depth = q_all.shape
    tokens = q_ref.shape[0]
    clusters = slots_ref.shape[2]
    owned = clusters // devices
    me = lax.axis_index("seq") * help_size + lax.axis_index("help")
    part = me // owners
    rank = lax.rem(me, owners)

    def place(index):
        return {"seq": index // help_size, "help": lax.rem(index, help_size)}

    def partner(step):
        return lax.rem(me + step, devices)

    def fellow(away, step):
        return (part + away) * owners + lax.rem(rank + step, owners)

    def columns(head):
        return pl.ds(pl.multiple_of(head * depth, depth), depth)

    def rows(index):
        return pl.ds(pl.multiple_of(index * tokens, tokens), tokens)

    def remote(source, landing, send_sem, recv_sem, target):
        return pltpu.make_async_remote_copy(
            src_ref=source,
            dst_ref=landing,
            send_sem=send_sem,
            recv_sem=recv_sem,
            device_id=place(target),
            device_id_type=pl.DeviceIdType.MESH,
        )

    barrier = pltpu.get_barrier_semaphore()
    for step in range(1, devices):
        pl.semaphore_signal(
            barrier, inc=1, device_id=place(partner(step)), device_id_type=pl.DeviceIdType.MESH
        )

    sources = (k_ref, v_ref, q_ref, g_ref)
    landings = (k_all, v_all, q_all, g_all)

    def head_in(item, inner, source, target):
        return remote(
            sources[item].at[:, columns(lax.rem(target, owners) * share + inner)],
            landings[item].at[inner, rows(source)],
            send_in.at[inner, target, item],
            recv_in.at[inner, source, item],
            target,
        )

    def ids_in(source, target):
        first = lax.rem(target, owners) * share
        return remote(
            ids_ref.at[pl.ds(first, share)],
            ids_all.at[source],
            send_ids.at[target],
            recv_ids.at[source],
            target,
        )

    def own_in(item, inner):
        return pltpu.make_async_copy(
            sources[item].at[:, columns(rank * share + inner)],
            landings[item].at[inner, rows(me)],
            send_in.at[inner, me, item],
        )

    own_ids = pltpu.make_async_copy(
        ids_ref.at[pl.ds(rank * share, share)], ids_all.at[me], send_ids.at[me]
    )
    own_ids.start()
    for inner in range(share):
        for item in range(4):
            own_in(item, inner).start()
    pl.semaphore_wait(barrier, devices - 1)

    for away in range(1, parts):

        @pl.when(part + away < parts)
        def _():
            for step in range(owners):
                ids_in(me, fellow(away, step)).start()

    for step in range(1, owners):
        ids_in(me, fellow(0, step)).start()
    for inner in range(share):
        for away in range(1, parts):

            @pl.when(part + away < parts)
            def _():
                for step in range(owners):
                    for item in range(2):
                        head_in(item, inner, me, fellow(away, step)).start()

        for step in range(1, owners):
            for item in range(4):
                head_in(item, inner, me, fellow(0, step)).start()

    stages = (att_stage, dq_stage, dk_stage, dv_stage)
    results = (att_ref, dq_ref, dk_ref, dv_ref)
    fars = (dk_far_ref, dv_far_ref)

    def head_out(item, inner, owner, target):
        return remote(
            stages[item].at[inner, rows(target)],
            results[item].at[:, columns(lax.rem(owner, owners) * share + inner)],
            send_out.at[inner, target, item],
            recv_out.at[inner, owner, item],
            target,
        )

    def far_out(item, inner, owner, target):
        return remote(
            stages[2 + item].at[inner, rows(target)],
            fars[item].at[:, columns(lax.rem(owner, owners) * share + inner)],
            send_out.at[inner, target, 2 + item],
            recv_out.at[inner, owner, 2 + item],
            target,
        )

    def own_out(item, inner):
        return pltpu.make_async_copy(
            stages[item].at[inner, rows(me)],
            results[item].at[:, columns(rank * share + inner)],
            send_out.at[inner, me, item],
        )

    def sums_slice(target):
        return pl.ds(pl.multiple_of(target * owned, owned), owned)

    def sums_out(inner, owner, target):
        return remote(
            sums_stage.at[inner, sums_slice(target)],
            sums_ref.at[lax.rem(owner, owners) * share + inner],
            send_sums.at[inner, target],
            recv_sums.at[inner, owner],
            target,
        )

    def own_sums(inner):
        return pltpu.make_async_copy(
            sums_stage.at[inner, sums_slice(me)],
            sums_ref.at[rank * share + inner],
            send_sums.at[inner, me],
        )

    scale = depth ** (-0.5)
    group = 2 if owners % 2 == 0 else 1
    block = group * tokens
    earlier = lax.broadcasted_iota(jnp.int32, (block, block), 1) <= lax.broadcasted_iota(
        jnp.int32, (block, block), 0
    )

    def attend(inner, first, last, label_row, label_columns):
        for index in reversed(range(first, last)):
            low, high = index * block, (index + 1) * block
            query, grad = q_all[inner, low:high], g_all[inner, low:high]
            keys, values = k_all[inner, :high], v_all[inner, :high]
            label_column = jnp.concatenate(
                label_columns[index * group : (index + 1) * group], axis=0
            )
            allowed = label_column == label_row[:, :high]
            near = allowed[:, low:] & earlier
            allowed = near if low == 0 else jnp.concatenate([allowed[:, :low], near], axis=1)
            scores = (
                lax.dot_general(
                    query, keys, (((1,), (1,)), ((), ())), preferred_element_type=jnp.float32
                )
                * scale
            )
            scores = jnp.where(allowed, scores, MASKED)
            peak = jnp.max(scores, axis=1, keepdims=True)
            weights = jnp.exp(scores - peak)
            weights = weights * (1.0 / jnp.sum(weights, axis=1, keepdims=True))
            weights_low = weights.astype(jnp.bfloat16)
            context = jnp.dot(weights_low, values, preferred_element_type=jnp.float32)
            grad_weights = lax.dot_general(
                grad, values, (((1,), (1,)), ((), ())), preferred_element_type=jnp.float32
            )
            delta = jnp.sum(grad.astype(jnp.float32) * context, axis=1, keepdims=True)
            grad_scores = (weights * (grad_weights - delta)).astype(jnp.bfloat16)
            att_stage[inner, low:high] = context.astype(jnp.bfloat16)
            dq_stage[inner, low:high] = (
                jnp.dot(grad_scores, keys, preferred_element_type=jnp.float32) * scale
            ).astype(jnp.bfloat16)
            dv_more = lax.dot_general(
                weights_low, grad, (((0,), (0,)), ((), ())), preferred_element_type=jnp.float32
            )
            dk_more = lax.dot_general(
                grad_scores, query, (((0,), (0,)), ((), ())), preferred_element_type=jnp.float32
            )
            if index == last - 1:
                dv_total[:high] = dv_more
                dk_total[:high] = dk_more
            else:
                dv_total[:high] += dv_more
                dk_total[:high] += dk_more
        end = last * block
        dk_stage[inner, :end] = (dk_total[:end] * scale).astype(jnp.bfloat16)
        dv_stage[inner, :end] = dv_total[:end].astype(jnp.bfloat16)

    def key_sums(inner, label_row):
        key_float = k_all[inner].astype(jnp.float32)
        spread = jnp.mean(key_float * key_float, axis=1, keepdims=True)
        units = key_float * (lax.rsqrt(spread + 1e-06) * scale)
        units_high = units.astype(jnp.bfloat16)
        units_rest = (units - units_high.astype(jnp.float32)).astype(jnp.bfloat16)
        numbers = lax.broadcasted_iota(jnp.int32, (clusters, 1), 0)
        named = (numbers.astype(jnp.float32) == label_row).astype(jnp.bfloat16)
        owner_of = (numbers == slots_ref[rank * share + inner]).astype(jnp.bfloat16)
        chosen = jnp.dot(owner_of, named, preferred_element_type=jnp.float32).astype(jnp.bfloat16)
        sums_stage[inner] = jnp.dot(
            chosen, units_high, preferred_element_type=jnp.float32
        ) + jnp.dot(chosen, units_rest, preferred_element_type=jnp.float32)

    own_ids.wait()
    for step in range(1, owners):
        ids_in(fellow(0, step), me).wait_recv()

    for mine in range(parts):

        @pl.when(part == mine)
        def _():
            first, last = mine * owners // group, (mine + 1) * owners // group
            before = mine * owners
            for source in range(before):
                ids_in(source, me).wait_recv()
            for inner in range(share):
                labels = [
                    ids_all[index, inner].astype(jnp.float32) for index in range(before + owners)
                ]
                label_row = jnp.concatenate(labels, axis=1)
                label_columns = [
                    jnp.transpose(jnp.broadcast_to(label, (tokens, tokens)))[:, :1]
                    for label in labels
                ]
                for item in range(4):
                    own_in(item, inner).wait()
                    for step in range(1, owners):
                        head_in(item, inner, fellow(0, step), me).wait_recv()
                for item in range(2):
                    for source in range(before):
                        head_in(item, inner, source, me).wait_recv()
                attend(inner, first, last, label_row, label_columns)
                for target in range(before):
                    for item in range(2):
                        far_out(item, inner, me, target).start()
                for step in range(1, owners):
                    for item in range(4):
                        head_out(item, inner, me, fellow(0, step)).start()
                for item in range(4):
                    own_out(item, inner).start()
                if mine == parts - 1:
                    key_sums(inner, label_row)
                    for step in range(1, devices):
                        sums_out(inner, me, partner(step)).start()
                    own_sums(inner).start()
            for target in range(before):
                for inner in range(share):
                    for item in range(2):
                        far_out(item, inner, me, target).wait_send()
            for inner in range(share):
                if mine == parts - 1:
                    for step in range(1, devices):
                        sums_out(inner, me, partner(step)).wait_send()
                    own_sums(inner).wait()
                    for step in range(1, owners):
                        sums_out(inner, fellow(0, step), me).wait_recv()
                else:
                    for step in range(owners):
                        sums_out(inner, (parts - 1) * owners + step, me).wait_recv()

    for away in range(1, parts):

        @pl.when(part + away < parts)
        def _():
            for step in range(owners):
                ids_in(me, fellow(away, step)).wait_send()
                for inner in range(share):
                    for item in range(2):
                        head_in(item, inner, me, fellow(away, step)).wait_send()
                        far_out(item, inner, fellow(away, step), me).wait_recv()

    for step in range(1, owners):
        ids_in(me, fellow(0, step)).wait_send()
        for inner in range(share):
            for item in range(4):
                head_in(item, inner, me, fellow(0, step)).wait_send()
                head_out(item, inner, me, fellow(0, step)).wait_send()
                head_out(item, inner, fellow(0, step), me).wait_recv()
    for inner in range(share):
        for item in range(4):
            own_out(item, inner).wait()


def finish_kernel(
    help_size,
    owners,
    parts,
    att_ref,
    dq_ref,
    dk_ref,
    dv_ref,
    dk_far_ref,
    dv_far_ref,
    sums_ref,
    att_out,
    dq_out,
    dk_out,
    dv_out,
    sums_out,
):
    me = lax.axis_index("seq") * help_size + lax.axis_index("help")
    has_far = me // owners + 1 < parts
    att_out[...] = att_ref[...]
    dq_out[...] = dq_ref[...]
    sums_out[...] = sums_ref[...]
    for near, far, out in ((dk_ref, dk_far_ref, dk_out), (dv_ref, dv_far_ref, dv_out)):
        more = jnp.where(has_far, far[...].astype(jnp.float32), 0.0)
        out[...] = (near[...].astype(jnp.float32) + more).astype(out.dtype)


def routed_by_head(query_rows, key_rows, value_rows, out_grad, cluster_ids, cluster_slots):
    token_count, width = query_rows.shape
    local_heads, cluster_total = cluster_slots.shape
    depth = width // local_heads
    seq_size, help_size = lax.axis_size("seq"), lax.axis_size("help")
    devices = seq_size * help_size
    parts = 2
    owners = devices // parts
    if devices != local_heads or seq_size % parts or token_count != depth:
        return local(query_rows, key_rows, value_rows, out_grad, cluster_ids, cluster_slots)
    share = local_heads // owners
    total = devices * token_count
    low = jnp.bfloat16
    full = (share, total, depth)
    sums_shape = jax.ShapeDtypeStruct(
        (local_heads, cluster_total // devices, depth), jnp.float32
    )
    rows_shape = jax.ShapeDtypeStruct((token_count, width), low)
    landed = pl.pallas_call(
        functools.partial(head_kernel, seq_size, help_size, parts),
        out_shape=[rows_shape] * 6 + [sums_shape],
        in_specs=[pl.BlockSpec(memory_space=pltpu.HBM)] * 4
        + [pl.BlockSpec(memory_space=pltpu.VMEM)] * 2,
        out_specs=[pl.BlockSpec(memory_space=pl.ANY)] * 7,
        scratch_shapes=[pltpu.VMEM(full, low)] * 4
        + [pltpu.VMEM((devices, share, 1, token_count), jnp.int32)]
        + [pltpu.VMEM(full, low)] * 4
        + [pltpu.VMEM((share, cluster_total, depth), jnp.float32)]
        + [pltpu.VMEM((total, depth), jnp.float32)] * 2
        + [pltpu.SemaphoreType.DMA((share, devices, 4))] * 2
        + [pltpu.SemaphoreType.DMA((devices,))] * 2
        + [pltpu.SemaphoreType.DMA((share, devices, 4))] * 2
        + [pltpu.SemaphoreType.DMA((share, devices))] * 2,
        compiler_params=pltpu.CompilerParams(
            collective_id=0, has_side_effects=True, vmem_limit_bytes=40 * 1024 * 1024
        ),
    )(
        query_rows,
        key_rows,
        value_rows,
        out_grad,
        cluster_ids.reshape(local_heads, 1, token_count),
        cluster_slots.reshape(local_heads, 1, cluster_total),
    )
    return tuple(
        pl.pallas_call(
            functools.partial(finish_kernel, help_size, owners, parts),
            out_shape=[rows_shape] * 4 + [sums_shape],
            in_specs=[pl.BlockSpec(memory_space=pltpu.VMEM)] * 7,
            out_specs=[pl.BlockSpec(memory_space=pltpu.VMEM)] * 5,
            compiler_params=pltpu.CompilerParams(vmem_limit_bytes=16 * 1024 * 1024),
        )(*landed)
    )


def solution(mesh):
    in_specs = (
        P(("groups", "seq", "help"), "head"),
        P(("groups", "seq", "help"), "head"),
        P(("groups", "seq", "help"), "head"),
        P(("groups", "seq", "help"), "head"),
        P("head", ("groups", "seq", "help"), None),
        P(("groups", "head"), None),
    )
    out_specs = (
        P(("groups", "seq", "help"), "head"),
        P(("groups", "seq", "help"), "head"),
        P(("groups", "seq", "help"), "head"),
        P(("groups", "seq", "help"), "head"),
        P(("groups", "head"), ("seq", "help"), None),
    )
    return jax.shard_map(routed_by_head, mesh=mesh, in_specs=in_specs, out_specs=out_specs, check_vma=False)
```

```python
import functools

import jax
import jax.numpy as jnp
from jax import lax
from jax.experimental import pallas as pl
from jax.experimental.pallas import tpu as pltpu
from jax.sharding import PartitionSpec as P

BLK = 256
MOST = 2


def unit_keys(key_part):
    key_float = key_part.astype(jnp.float32)
    spread = jnp.mean(key_float * key_float, axis=-1, keepdims=True)
    return key_float * lax.rsqrt(spread + 1e-06) * key_part.shape[-1] ** (-0.5)


def cluster_attention(packed_rows, token_pos):
    depth = packed_rows.shape[-1] // 4
    count = packed_rows.shape[0]
    query_part = packed_rows[:, :depth]
    key_part = packed_rows[:, depth : 2 * depth]
    value_part = packed_rows[:, 2 * depth : 3 * depth]
    grad_part = packed_rows[:, 3 * depth :]
    valid = token_pos >= 0
    rank = jnp.cumsum(valid.astype(jnp.int32)) - 1
    block_id = rank // BLK
    allowed = valid[:, None] & valid[None, :] & (block_id[:, None] == block_id[None, :])
    allowed = allowed & (token_pos[None, :] <= token_pos[:, None])
    allowed = allowed | jnp.eye(count, dtype=bool)
    scale = depth ** (-0.5)
    scores = (
        lax.dot_general(
            query_part, key_part, (((1,), (1,)), ((), ())), preferred_element_type=jnp.float32
        )
        * scale
    )
    scores = jnp.where(allowed, scores, -1e30)
    peak = jnp.max(scores, axis=1, keepdims=True)
    weights = jnp.exp(scores - peak)
    weights = weights / jnp.sum(weights, axis=1, keepdims=True)
    weights_low = weights.astype(jnp.bfloat16)
    context = jnp.dot(weights_low, value_part, preferred_element_type=jnp.float32)
    grad_value = lax.dot_general(
        weights_low, grad_part, (((0,), (0,)), ((), ())), preferred_element_type=jnp.float32
    )
    grad_weights = lax.dot_general(
        grad_part, value_part, (((1,), (1,)), ((), ())), preferred_element_type=jnp.float32
    )
    delta = jnp.sum(grad_part.astype(jnp.float32) * context, axis=1, keepdims=True)
    grad_scores = (weights * (grad_weights - delta)).astype(jnp.bfloat16)
    grad_query = jnp.dot(grad_scores, key_part, preferred_element_type=jnp.float32) * scale
    grad_key = (
        lax.dot_general(
            grad_scores, query_part, (((0,), (0,)), ((), ())), preferred_element_type=jnp.float32
        )
        * scale
    )
    return jnp.concatenate([context, grad_query, grad_key, grad_value], axis=1).astype(jnp.bfloat16)


def owner_work(arrived, arrived_pos):
    head_count, per_device, source_count, most_count, packed_width = arrived.shape
    flat_rows = arrived.reshape(head_count, per_device, source_count * most_count, packed_width)
    flat_pos = arrived_pos.reshape(head_count, per_device, source_count * most_count)

    def one_head(head_pair):
        return jax.vmap(cluster_attention)(head_pair[0], head_pair[1])

    results = lax.map(one_head, (flat_rows, flat_pos)).reshape(arrived.shape)
    owner_sums = jnp.zeros((head_count, 1), jnp.float32)
    return (results, owner_sums)


def local(query_rows, key_rows, value_rows, out_grad, cluster_ids, cluster_slots):
    token_count, width = query_rows.shape
    local_heads, cluster_total = cluster_slots.shape
    depth = width // local_heads
    seq_size = lax.axis_size("seq")
    help_size = lax.axis_size("help")
    device_count = seq_size * help_size
    per_device = cluster_total // device_count
    packed = jnp.concatenate(
        [
            piece.reshape(token_count, local_heads, depth)
            for piece in (query_rows, key_rows, value_rows, out_grad)
        ],
        axis=2,
    )
    packed = packed.transpose(1, 0, 2)
    labels = cluster_ids[:, :, 0]
    matches = labels[:, :, None] == jnp.arange(cluster_total, dtype=jnp.int32)[None, None, :]
    slot_of = jnp.sum(jnp.where(matches, cluster_slots[:, None, :], 0), axis=2)
    positions = jnp.arange(token_count, dtype=jnp.int32)
    earlier = (labels[:, :, None] == labels[:, None, :]) & (
        positions[None, None, :] < positions[None, :, None]
    )
    within = jnp.sum(earlier.astype(jnp.int32), axis=2)
    target = slot_of // per_device
    column = slot_of % per_device
    flat_slot = (column * device_count + target) * MOST + within
    slot_total = per_device * device_count * MOST
    head_index = jnp.arange(local_heads, dtype=jnp.int32)[:, None]
    send_rows = (
        jnp.zeros((local_heads, slot_total, 4 * depth), jnp.bfloat16)
        .at[head_index, flat_slot]
        .set(packed)
    )
    global_pos = lax.axis_index(("seq", "help")) * token_count + positions
    send_pos = (
        jnp.full((local_heads, slot_total), -1, jnp.int32)
        .at[head_index, flat_slot]
        .set(jnp.broadcast_to(global_pos, (local_heads, token_count)))
    )
    grid_rows = (local_heads, per_device, device_count, MOST, 4 * depth)
    results, owner_sums = owner_work(
        lax.all_to_all(
            send_rows.reshape(grid_rows), ("seq", "help"), split_axis=2, concat_axis=2, tiled=True
        ),
        lax.all_to_all(
            send_pos.reshape(grid_rows[:-1]),
            ("seq", "help"),
            split_axis=2,
            concat_axis=2,
            tiled=True,
        ),
    )
    returned, owner_sums = (
        lax.all_to_all(results, ("seq", "help"), split_axis=2, concat_axis=2, tiled=True),
        owner_sums,
    )
    gathered = returned.reshape(local_heads, slot_total, 4 * depth)[head_index, flat_slot]
    gathered = gathered.transpose(1, 0, 2)
    pieces = [
        gathered[:, :, index * depth : (index + 1) * depth].reshape(token_count, width)
        for index in range(4)
    ]
    units = unit_keys(packed[:, :, depth : 2 * depth])
    chosen = (
        slot_of[:, :, None]
        == jnp.arange(lax.axis_size(("seq", "help")) * per_device, dtype=jnp.int32)[None, None, :]
    )
    centroid_sums = lax.psum_scatter(
        jnp.einsum(
            "htc,htd->chd", chosen.astype(jnp.float32), units, precision=lax.Precision.HIGHEST
        ),
        ("seq", "help"),
        scatter_dimension=0,
        tiled=True,
    ).transpose(1, 0, 2)
    return (pieces[0], pieces[1], pieces[2], pieces[3], centroid_sums)


MASKED = -1e30


def head_kernel(
    seq_size,
    help_size,
    parts,
    q_ref,
    k_ref,
    v_ref,
    g_ref,
    ids_ref,
    slots_ref,
    att_ref,
    dq_ref,
    dk_ref,
    dv_ref,
    dk_far_ref,
    dv_far_ref,
    sums_ref,
    q_all,
    k_all,
    v_all,
    g_all,
    ids_all,
    att_stage,
    dq_stage,
    dk_stage,
    dv_stage,
    sums_stage,
    dk_total,
    dv_total,
    send_in,
    recv_in,
    send_ids,
    recv_ids,
    send_out,
    recv_out,
    send_sums,
    recv_sums,
):
    devices = seq_size * help_size
    owners = devices // parts
    share, _, depth = q_all.shape
    tokens = q_ref.shape[0]
    clusters = slots_ref.shape[2]
    owned = clusters // devices
    me = lax.axis_index("seq") * help_size + lax.axis_index("help")
    part = me // owners
    rank = lax.rem(me, owners)

    def place(index):
        return {"seq": index // help_size, "help": lax.rem(index, help_size)}

    def partner(step):
        return lax.rem(me + step, devices)

    def fellow(away, step):
        return (part + away) * owners + lax.rem(rank + step, owners)

    def columns(head):
        return pl.ds(pl.multiple_of(head * depth, depth), depth)

    def rows(index):
        return pl.ds(pl.multiple_of(index * tokens, tokens), tokens)

    def remote(source, landing, send_sem, recv_sem, target):
        return pltpu.make_async_remote_copy(
            src_ref=source,
            dst_ref=landing,
            send_sem=send_sem,
            recv_sem=recv_sem,
            device_id=place(target),
            device_id_type=pl.DeviceIdType.MESH,
        )

    barrier = pltpu.get_barrier_semaphore()
    for step in range(1, devices):
        pl.semaphore_signal(
            barrier, inc=1, device_id=place(partner(step)), device_id_type=pl.DeviceIdType.MESH
        )

    sources = (k_ref, v_ref, q_ref, g_ref)
    landings = (k_all, v_all, q_all, g_all)

    def head_in(item, inner, source, target):
        return remote(
            sources[item].at[:, columns(lax.rem(target, owners) * share + inner)],
            landings[item].at[inner, rows(source)],
            send_in.at[inner, target, item],
            recv_in.at[inner, source, item],
            target,
        )

    def ids_in(source, target):
        first = lax.rem(target, owners) * share
        return remote(
            ids_ref.at[pl.ds(first, share)],
            ids_all.at[source],
            send_ids.at[target],
            recv_ids.at[source],
            target,
        )

    def own_in(item, inner):
        return pltpu.make_async_copy(
            sources[item].at[:, columns(rank * share + inner)],
            landings[item].at[inner, rows(me)],
            send_in.at[inner, me, item],
        )

    own_ids = pltpu.make_async_copy(
        ids_ref.at[pl.ds(rank * share, share)], ids_all.at[me], send_ids.at[me]
    )
    own_ids.start()
    for inner in range(share):
        for item in range(4):
            own_in(item, inner).start()
    pl.semaphore_wait(barrier, devices - 1)

    for away in range(1, parts):

        @pl.when(part + away < parts)
        def _():
            for step in range(owners):
                ids_in(me, fellow(away, step)).start()

    for step in range(1, owners):
        ids_in(me, fellow(0, step)).start()
    for inner in range(share):
        for away in range(1, parts):

            @pl.when(part + away < parts)
            def _():
                for step in range(owners):
                    for item in range(2):
                        head_in(item, inner, me, fellow(away, step)).start()

        for step in range(1, owners):
            for item in range(4):
                head_in(item, inner, me, fellow(0, step)).start()

    stages = (att_stage, dq_stage, dk_stage, dv_stage)
    results = (att_ref, dq_ref, dk_ref, dv_ref)
    fars = (dk_far_ref, dv_far_ref)

    def head_out(item, inner, owner, target):
        return remote(
            stages[item].at[inner, rows(target)],
            results[item].at[:, columns(lax.rem(owner, owners) * share + inner)],
            send_out.at[inner, target, item],
            recv_out.at[inner, owner, item],
            target,
        )

    def far_out(item, inner, owner, target):
        return remote(
            stages[2 + item].at[inner, rows(target)],
            fars[item].at[:, columns(lax.rem(owner, owners) * share + inner)],
            send_out.at[inner, target, 2 + item],
            recv_out.at[inner, owner, 2 + item],
            target,
        )

    def own_out(item, inner):
        return pltpu.make_async_copy(
            stages[item].at[inner, rows(me)],
            results[item].at[:, columns(rank * share + inner)],
            send_out.at[inner, me, item],
        )

    def sums_slice(target):
        return pl.ds(pl.multiple_of(target * owned, owned), owned)

    def sums_out(inner, owner, target):
        return remote(
            sums_stage.at[inner, sums_slice(target)],
            sums_ref.at[lax.rem(owner, owners) * share + inner],
            send_sums.at[inner, target],
            recv_sums.at[inner, owner],
            target,
        )

    def own_sums(inner):
        return pltpu.make_async_copy(
            sums_stage.at[inner, sums_slice(me)],
            sums_ref.at[rank * share + inner],
            send_sums.at[inner, me],
        )

    scale = depth ** (-0.5)
    group = 2 if owners % 2 == 0 else 1
    block = group * tokens
    earlier = lax.broadcasted_iota(jnp.int32, (block, block), 1) <= lax.broadcasted_iota(
        jnp.int32, (block, block), 0
    )

    def attend(inner, first, last, label_row, label_columns):
        for index in reversed(range(first, last)):
            low, high = index * block, (index + 1) * block
            query, grad = q_all[inner, low:high], g_all[inner, low:high]
            keys, values = k_all[inner, :high], v_all[inner, :high]
            label_column = jnp.concatenate(
                label_columns[index * group : (index + 1) * group], axis=0
            )
            allowed = label_column == label_row[:, :high]
            near = allowed[:, low:] & earlier
            allowed = near if low == 0 else jnp.concatenate([allowed[:, :low], near], axis=1)
            scores = (
                lax.dot_general(
                    query, keys, (((1,), (1,)), ((), ())), preferred_element_type=jnp.float32
                )
                * scale
            )
            scores = jnp.where(allowed, scores, MASKED)
            peak = jnp.max(scores, axis=1, keepdims=True)
            weights = jnp.exp(scores - peak)
            weights = weights * (1.0 / jnp.sum(weights, axis=1, keepdims=True))
            weights_low = weights.astype(jnp.bfloat16)
            context = jnp.dot(weights_low, values, preferred_element_type=jnp.float32)
            grad_weights = lax.dot_general(
                grad, values, (((1,), (1,)), ((), ())), preferred_element_type=jnp.float32
            )
            delta = jnp.sum(grad.astype(jnp.float32) * context, axis=1, keepdims=True)
            grad_scores = (weights * (grad_weights - delta)).astype(jnp.bfloat16)
            att_stage[inner, low:high] = context.astype(jnp.bfloat16)
            dq_stage[inner, low:high] = (
                jnp.dot(grad_scores, keys, preferred_element_type=jnp.float32) * scale
            ).astype(jnp.bfloat16)
            dv_more = lax.dot_general(
                weights_low, grad, (((0,), (0,)), ((), ())), preferred_element_type=jnp.float32
            )
            dk_more = lax.dot_general(
                grad_scores, query, (((0,), (0,)), ((), ())), preferred_element_type=jnp.float32
            )
            if index == last - 1:
                dv_total[:high] = dv_more
                dk_total[:high] = dk_more
            else:
                dv_total[:high] += dv_more
                dk_total[:high] += dk_more
        end = last * block
        dk_stage[inner, :end] = (dk_total[:end] * scale).astype(jnp.bfloat16)
        dv_stage[inner, :end] = dv_total[:end].astype(jnp.bfloat16)

    def key_sums(inner, label_row):
        key_float = k_all[inner].astype(jnp.float32)
        spread = jnp.mean(key_float * key_float, axis=1, keepdims=True)
        units = key_float * (lax.rsqrt(spread + 1e-06) * scale)
        units_high = units.astype(jnp.bfloat16)
        units_rest = (units - units_high.astype(jnp.float32)).astype(jnp.bfloat16)
        numbers = lax.broadcasted_iota(jnp.int32, (clusters, 1), 0)
        named = (numbers.astype(jnp.float32) == label_row).astype(jnp.bfloat16)
        owner_of = (numbers == slots_ref[rank * share + inner]).astype(jnp.bfloat16)
        chosen = jnp.dot(owner_of, named, preferred_element_type=jnp.float32).astype(jnp.bfloat16)
        sums_stage[inner] = jnp.dot(
            chosen, units_high, preferred_element_type=jnp.float32
        ) + jnp.dot(chosen, units_rest, preferred_element_type=jnp.float32)

    own_ids.wait()
    for step in range(1, owners):
        ids_in(fellow(0, step), me).wait_recv()

    for mine in range(parts):

        @pl.when(part == mine)
        def _():
            first, last = mine * owners // group, (mine + 1) * owners // group
            before = mine * owners
            for source in range(before):
                ids_in(source, me).wait_recv()
            for inner in range(share):
                labels = [
                    ids_all[index, inner].astype(jnp.float32) for index in range(before + owners)
                ]
                label_row = jnp.concatenate(labels, axis=1)
                label_columns = [
                    jnp.transpose(jnp.broadcast_to(label, (tokens, tokens)))[:, :1]
                    for label in labels
                ]
                for item in range(4):
                    own_in(item, inner).wait()
                    for step in range(1, owners):
                        head_in(item, inner, fellow(0, step), me).wait_recv()
                for item in range(2):
                    for source in range(before):
                        head_in(item, inner, source, me).wait_recv()
                attend(inner, first, last, label_row, label_columns)
                for target in range(before):
                    for item in range(2):
                        far_out(item, inner, me, target).start()
                for step in range(1, owners):
                    for item in range(4):
                        head_out(item, inner, me, fellow(0, step)).start()
                for item in range(4):
                    own_out(item, inner).start()
                if mine == parts - 1:
                    key_sums(inner, label_row)
                    for step in range(1, devices):
                        sums_out(inner, me, partner(step)).start()
                    own_sums(inner).start()
            for target in range(before):
                for inner in range(share):
                    for item in range(2):
                        far_out(item, inner, me, target).wait_send()
            for inner in range(share):
                if mine == parts - 1:
                    for step in range(1, devices):
                        sums_out(inner, me, partner(step)).wait_send()
                    own_sums(inner).wait()
                    for step in range(1, owners):
                        sums_out(inner, fellow(0, step), me).wait_recv()
                else:
                    for step in range(owners):
                        sums_out(inner, (parts - 1) * owners + step, me).wait_recv()

    for away in range(1, parts):

        @pl.when(part + away < parts)
        def _():
            for step in range(owners):
                ids_in(me, fellow(away, step)).wait_send()
                for inner in range(share):
                    for item in range(2):
                        head_in(item, inner, me, fellow(away, step)).wait_send()
                        far_out(item, inner, fellow(away, step), me).wait_recv()

    for step in range(1, owners):
        ids_in(me, fellow(0, step)).wait_send()
        for inner in range(share):
            for item in range(4):
                head_in(item, inner, me, fellow(0, step)).wait_send()
                head_out(item, inner, me, fellow(0, step)).wait_send()
                head_out(item, inner, fellow(0, step), me).wait_recv()
    for inner in range(share):
        for item in range(4):
            own_out(item, inner).wait()


def finish_kernel(
    help_size,
    owners,
    parts,
    att_ref,
    dq_ref,
    dk_ref,
    dv_ref,
    dk_far_ref,
    dv_far_ref,
    sums_ref,
    att_out,
    dq_out,
    dk_out,
    dv_out,
    sums_out,
):
    me = lax.axis_index("seq") * help_size + lax.axis_index("help")
    has_far = me // owners + 1 < parts
    att_out[...] = att_ref[...]
    dq_out[...] = dq_ref[...]
    sums_out[...] = sums_ref[...]
    for near, far, out in ((dk_ref, dk_far_ref, dk_out), (dv_ref, dv_far_ref, dv_out)):
        more = jnp.where(has_far, far[...].astype(jnp.float32), 0.0)
        out[...] = (near[...].astype(jnp.float32) + more).astype(out.dtype)


def routed_by_head(query_rows, key_rows, value_rows, out_grad, cluster_ids, cluster_slots):
    token_count, width = query_rows.shape
    local_heads, cluster_total = cluster_slots.shape
    depth = width // local_heads
    seq_size, help_size = lax.axis_size("seq"), lax.axis_size("help")
    devices = seq_size * help_size
    parts = 2
    owners = devices // parts
    if devices != local_heads or seq_size % parts or token_count != depth:
        return local(query_rows, key_rows, value_rows, out_grad, cluster_ids, cluster_slots)
    share = local_heads // owners
    total = devices * token_count
    low = jnp.bfloat16
    full = (share, total, depth)
    sums_shape = jax.ShapeDtypeStruct(
        (local_heads, cluster_total // devices, depth), jnp.float32
    )
    rows_shape = jax.ShapeDtypeStruct((token_count, width), low)
    landed = pl.pallas_call(
        functools.partial(head_kernel, seq_size, help_size, parts),
        out_shape=[rows_shape] * 6 + [sums_shape],
        in_specs=[pl.BlockSpec(memory_space=pltpu.HBM)] * 4
        + [pl.BlockSpec(memory_space=pltpu.VMEM)] * 2,
        out_specs=[pl.BlockSpec(memory_space=pl.ANY)] * 7,
        scratch_shapes=[pltpu.VMEM(full, low)] * 4
        + [pltpu.VMEM((devices, share, 1, token_count), jnp.int32)]
        + [pltpu.VMEM(full, low)] * 4
        + [pltpu.VMEM((share, cluster_total, depth), jnp.float32)]
        + [pltpu.VMEM((total, depth), jnp.float32)] * 2
        + [pltpu.SemaphoreType.DMA((share, devices, 4))] * 2
        + [pltpu.SemaphoreType.DMA((devices,))] * 2
        + [pltpu.SemaphoreType.DMA((share, devices, 4))] * 2
        + [pltpu.SemaphoreType.DMA((share, devices))] * 2,
        compiler_params=pltpu.CompilerParams(
            collective_id=0, has_side_effects=True, vmem_limit_bytes=60 * 1024 * 1024
        ),
    )(
        query_rows,
        key_rows,
        value_rows,
        out_grad,
        cluster_ids.reshape(local_heads, 1, token_count),
        cluster_slots.reshape(local_heads, 1, cluster_total),
    )
    return tuple(
        pl.pallas_call(
            functools.partial(finish_kernel, help_size, owners, parts),
            out_shape=[rows_shape] * 4 + [sums_shape],
            in_specs=[pl.BlockSpec(memory_space=pltpu.VMEM)] * 7,
            out_specs=[pl.BlockSpec(memory_space=pltpu.VMEM)] * 5,
            compiler_params=pltpu.CompilerParams(vmem_limit_bytes=60 * 1024 * 1024),
        )(*landed)
    )


def solution(mesh):
    in_specs = (
        P(("groups", "seq", "help"), "head"),
        P(("groups", "seq", "help"), "head"),
        P(("groups", "seq", "help"), "head"),
        P(("groups", "seq", "help"), "head"),
        P("head", ("groups", "seq", "help"), None),
        P(("groups", "head"), None),
    )
    out_specs = (
        P(("groups", "seq", "help"), "head"),
        P(("groups", "seq", "help"), "head"),
        P(("groups", "seq", "help"), "head"),
        P(("groups", "seq", "help"), "head"),
        P(("groups", "head"), ("seq", "help"), None),
    )
    return jax.shard_map(routed_by_head, mesh=mesh, in_specs=in_specs, out_specs=out_specs, check_vma=False)
```

```python
import functools

import jax
import jax.numpy as jnp
from jax import lax
from jax.experimental import pallas as pl
from jax.experimental.pallas import tpu as pltpu
from jax.sharding import PartitionSpec as P

BLK = 256
MOST = 2


def unit_keys(key_part):
    key_float = key_part.astype(jnp.float32)
    spread = jnp.mean(key_float * key_float, axis=-1, keepdims=True)
    return key_float * lax.rsqrt(spread + 1e-06) * key_part.shape[-1] ** (-0.5)


def cluster_attention(packed_rows, token_pos):
    depth = packed_rows.shape[-1] // 4
    count = packed_rows.shape[0]
    query_part = packed_rows[:, :depth]
    key_part = packed_rows[:, depth : 2 * depth]
    value_part = packed_rows[:, 2 * depth : 3 * depth]
    grad_part = packed_rows[:, 3 * depth :]
    valid = token_pos >= 0
    rank = jnp.cumsum(valid.astype(jnp.int32)) - 1
    block_id = rank // BLK
    allowed = valid[:, None] & valid[None, :] & (block_id[:, None] == block_id[None, :])
    allowed = allowed & (token_pos[None, :] <= token_pos[:, None])
    allowed = allowed | jnp.eye(count, dtype=bool)
    scale = depth ** (-0.5)
    scores = (
        lax.dot_general(
            query_part, key_part, (((1,), (1,)), ((), ())), preferred_element_type=jnp.float32
        )
        * scale
    )
    scores = jnp.where(allowed, scores, -1e30)
    peak = jnp.max(scores, axis=1, keepdims=True)
    weights = jnp.exp(scores - peak)
    weights = weights / jnp.sum(weights, axis=1, keepdims=True)
    weights_low = weights.astype(jnp.bfloat16)
    context = jnp.dot(weights_low, value_part, preferred_element_type=jnp.float32)
    grad_value = lax.dot_general(
        weights_low, grad_part, (((0,), (0,)), ((), ())), preferred_element_type=jnp.float32
    )
    grad_weights = lax.dot_general(
        grad_part, value_part, (((1,), (1,)), ((), ())), preferred_element_type=jnp.float32
    )
    delta = jnp.sum(grad_part.astype(jnp.float32) * context, axis=1, keepdims=True)
    grad_scores = (weights * (grad_weights - delta)).astype(jnp.bfloat16)
    grad_query = jnp.dot(grad_scores, key_part, preferred_element_type=jnp.float32) * scale
    grad_key = (
        lax.dot_general(
            grad_scores, query_part, (((0,), (0,)), ((), ())), preferred_element_type=jnp.float32
        )
        * scale
    )
    return jnp.concatenate([context, grad_query, grad_key, grad_value], axis=1).astype(jnp.bfloat16)


def owner_work(arrived, arrived_pos):
    head_count, per_device, source_count, most_count, packed_width = arrived.shape
    flat_rows = arrived.reshape(head_count, per_device, source_count * most_count, packed_width)
    flat_pos = arrived_pos.reshape(head_count, per_device, source_count * most_count)

    def one_head(head_pair):
        return jax.vmap(cluster_attention)(head_pair[0], head_pair[1])

    results = lax.map(one_head, (flat_rows, flat_pos)).reshape(arrived.shape)
    owner_sums = jnp.zeros((head_count, 1), jnp.float32)
    return (results, owner_sums)


def local(query_rows, key_rows, value_rows, out_grad, cluster_ids, cluster_slots):
    token_count, width = query_rows.shape
    local_heads, cluster_total = cluster_slots.shape
    depth = width // local_heads
    seq_size = lax.axis_size("seq")
    help_size = lax.axis_size("help")
    device_count = seq_size * help_size
    per_device = cluster_total // device_count
    packed = jnp.concatenate(
        [
            piece.reshape(token_count, local_heads, depth)
            for piece in (query_rows, key_rows, value_rows, out_grad)
        ],
        axis=2,
    )
    packed = packed.transpose(1, 0, 2)
    labels = cluster_ids[:, :, 0]
    matches = labels[:, :, None] == jnp.arange(cluster_total, dtype=jnp.int32)[None, None, :]
    slot_of = jnp.sum(jnp.where(matches, cluster_slots[:, None, :], 0), axis=2)
    positions = jnp.arange(token_count, dtype=jnp.int32)
    earlier = (labels[:, :, None] == labels[:, None, :]) & (
        positions[None, None, :] < positions[None, :, None]
    )
    within = jnp.sum(earlier.astype(jnp.int32), axis=2)
    target = slot_of // per_device
    column = slot_of % per_device
    flat_slot = (column * device_count + target) * MOST + within
    slot_total = per_device * device_count * MOST
    head_index = jnp.arange(local_heads, dtype=jnp.int32)[:, None]
    send_rows = (
        jnp.zeros((local_heads, slot_total, 4 * depth), jnp.bfloat16)
        .at[head_index, flat_slot]
        .set(packed)
    )
    global_pos = lax.axis_index(("seq", "help")) * token_count + positions
    send_pos = (
        jnp.full((local_heads, slot_total), -1, jnp.int32)
        .at[head_index, flat_slot]
        .set(jnp.broadcast_to(global_pos, (local_heads, token_count)))
    )
    grid_rows = (local_heads, per_device, device_count, MOST, 4 * depth)
    results, owner_sums = owner_work(
        lax.all_to_all(
            send_rows.reshape(grid_rows), ("seq", "help"), split_axis=2, concat_axis=2, tiled=True
        ),
        lax.all_to_all(
            send_pos.reshape(grid_rows[:-1]),
            ("seq", "help"),
            split_axis=2,
            concat_axis=2,
            tiled=True,
        ),
    )
    returned, owner_sums = (
        lax.all_to_all(results, ("seq", "help"), split_axis=2, concat_axis=2, tiled=True),
        owner_sums,
    )
    gathered = returned.reshape(local_heads, slot_total, 4 * depth)[head_index, flat_slot]
    gathered = gathered.transpose(1, 0, 2)
    pieces = [
        gathered[:, :, index * depth : (index + 1) * depth].reshape(token_count, width)
        for index in range(4)
    ]
    units = unit_keys(packed[:, :, depth : 2 * depth])
    chosen = (
        slot_of[:, :, None]
        == jnp.arange(lax.axis_size(("seq", "help")) * per_device, dtype=jnp.int32)[None, None, :]
    )
    centroid_sums = lax.psum_scatter(
        jnp.einsum(
            "htc,htd->chd", chosen.astype(jnp.float32), units, precision=lax.Precision.HIGHEST
        ),
        ("seq", "help"),
        scatter_dimension=0,
        tiled=True,
    ).transpose(1, 0, 2)
    return (pieces[0], pieces[1], pieces[2], pieces[3], centroid_sums)


MASKED = -1e30


def head_kernel(
    seq_size,
    help_size,
    parts,
    q_ref,
    k_ref,
    v_ref,
    g_ref,
    ids_ref,
    slots_ref,
    att_ref,
    dq_ref,
    dk_ref,
    dv_ref,
    dk_far_ref,
    dv_far_ref,
    sums_ref,
    q_all,
    k_all,
    v_all,
    g_all,
    ids_all,
    att_stage,
    dq_stage,
    dk_stage,
    dv_stage,
    sums_stage,
    dk_total,
    dv_total,
    send_in,
    recv_in,
    send_ids,
    recv_ids,
    send_out,
    recv_out,
    send_sums,
    recv_sums,
):
    devices = seq_size * help_size
    owners = devices // parts
    share, _, depth = q_all.shape
    tokens = q_ref.shape[0]
    clusters = slots_ref.shape[2]
    owned = clusters // devices
    me = lax.axis_index("seq") * help_size + lax.axis_index("help")
    part = me // owners
    rank = lax.rem(me, owners)

    def place(index):
        return {"seq": index // help_size, "help": lax.rem(index, help_size)}

    def partner(step):
        return lax.rem(me + step, devices)

    def fellow(away, step):
        return (part + away) * owners + lax.rem(rank + step, owners)

    def columns(head):
        return pl.ds(pl.multiple_of(head * depth, depth), depth)

    def rows(index):
        return pl.ds(pl.multiple_of(index * tokens, tokens), tokens)

    def remote(source, landing, send_sem, recv_sem, target):
        return pltpu.make_async_remote_copy(
            src_ref=source,
            dst_ref=landing,
            send_sem=send_sem,
            recv_sem=recv_sem,
            device_id=place(target),
            device_id_type=pl.DeviceIdType.MESH,
        )

    barrier = pltpu.get_barrier_semaphore()
    for step in range(1, devices):
        pl.semaphore_signal(
            barrier, inc=1, device_id=place(partner(step)), device_id_type=pl.DeviceIdType.MESH
        )

    sources = (k_ref, v_ref, q_ref, g_ref)
    landings = (k_all, v_all, q_all, g_all)

    def head_in(item, inner, source, target):
        return remote(
            sources[item].at[:, columns(lax.rem(target, owners) * share + inner)],
            landings[item].at[inner, rows(source)],
            send_in.at[inner, target, item],
            recv_in.at[inner, source, item],
            target,
        )

    def ids_in(source, target):
        first = lax.rem(target, owners) * share
        return remote(
            ids_ref.at[pl.ds(first, share)],
            ids_all.at[source],
            send_ids.at[target],
            recv_ids.at[source],
            target,
        )

    def own_in(item, inner):
        return pltpu.make_async_copy(
            sources[item].at[:, columns(rank * share + inner)],
            landings[item].at[inner, rows(me)],
            send_in.at[inner, me, item],
        )

    own_ids = pltpu.make_async_copy(
        ids_ref.at[pl.ds(rank * share, share)], ids_all.at[me], send_ids.at[me]
    )
    own_ids.start()
    for inner in range(share):
        for item in range(4):
            own_in(item, inner).start()
    pl.semaphore_wait(barrier, devices - 1)

    for away in range(1, parts):

        @pl.when(part + away < parts)
        def _():
            for step in range(owners):
                ids_in(me, fellow(away, step)).start()

    for step in range(1, owners):
        ids_in(me, fellow(0, step)).start()
    for inner in range(share):
        for away in range(1, parts):

            @pl.when(part + away < parts)
            def _():
                for step in range(owners):
                    for item in range(2):
                        head_in(item, inner, me, fellow(away, step)).start()

        for step in range(1, owners):
            for item in range(4):
                head_in(item, inner, me, fellow(0, step)).start()

    stages = (att_stage, dq_stage, dk_stage, dv_stage)
    results = (att_ref, dq_ref, dk_ref, dv_ref)
    fars = (dk_far_ref, dv_far_ref)

    def head_out(item, inner, owner, target):
        return remote(
            stages[item].at[inner, rows(target)],
            results[item].at[:, columns(lax.rem(owner, owners) * share + inner)],
            send_out.at[inner, target, item],
            recv_out.at[inner, owner, item],
            target,
        )

    def far_out(item, inner, owner, target):
        return remote(
            stages[2 + item].at[inner, rows(target)],
            fars[item].at[:, columns(lax.rem(owner, owners) * share + inner)],
            send_out.at[inner, target, 2 + item],
            recv_out.at[inner, owner, 2 + item],
            target,
        )

    def own_out(item, inner):
        return pltpu.make_async_copy(
            stages[item].at[inner, rows(me)],
            results[item].at[:, columns(rank * share + inner)],
            send_out.at[inner, me, item],
        )

    def sums_slice(target):
        return pl.ds(pl.multiple_of(target * owned, owned), owned)

    def sums_out(inner, owner, target):
        return remote(
            sums_stage.at[inner, sums_slice(target)],
            sums_ref.at[lax.rem(owner, owners) * share + inner],
            send_sums.at[inner, target],
            recv_sums.at[inner, owner],
            target,
        )

    def own_sums(inner):
        return pltpu.make_async_copy(
            sums_stage.at[inner, sums_slice(me)],
            sums_ref.at[rank * share + inner],
            send_sums.at[inner, me],
        )

    scale = depth ** (-0.5)
    group = 2 if owners % 2 == 0 else 1
    block = group * tokens
    earlier = lax.broadcasted_iota(jnp.int32, (block, block), 1) <= lax.broadcasted_iota(
        jnp.int32, (block, block), 0
    )

    def attend(inner, first, last, label_row, label_columns):
        for index in reversed(range(first, last)):
            low, high = index * block, (index + 1) * block
            query, grad = q_all[inner, low:high], g_all[inner, low:high]
            keys, values = k_all[inner, :high], v_all[inner, :high]
            label_column = jnp.concatenate(
                label_columns[index * group : (index + 1) * group], axis=0
            )
            allowed = label_column == label_row[:, :high]
            near = allowed[:, low:] & earlier
            allowed = near if low == 0 else jnp.concatenate([allowed[:, :low], near], axis=1)
            scores = (
                lax.dot_general(
                    query, keys, (((1,), (1,)), ((), ())), preferred_element_type=jnp.float32
                )
                * scale
            )
            scores = jnp.where(allowed, scores, MASKED)
            peak = jnp.max(scores, axis=1, keepdims=True)
            weights = jnp.exp(scores - peak)
            weights = weights * (1.0 / jnp.sum(weights, axis=1, keepdims=True))
            weights_low = weights.astype(jnp.bfloat16)
            context = jnp.dot(weights_low, values, preferred_element_type=jnp.float32)
            grad_weights = lax.dot_general(
                grad, values, (((1,), (1,)), ((), ())), preferred_element_type=jnp.float32
            )
            delta = jnp.sum(grad.astype(jnp.float32) * context, axis=1, keepdims=True)
            grad_scores = (weights * (grad_weights - delta)).astype(jnp.bfloat16)
            att_stage[inner, low:high] = context.astype(jnp.bfloat16)
            dq_stage[inner, low:high] = (
                jnp.dot(grad_scores, keys, preferred_element_type=jnp.float32) * scale
            ).astype(jnp.bfloat16)
            dv_more = lax.dot_general(
                weights_low, grad, (((0,), (0,)), ((), ())), preferred_element_type=jnp.float32
            )
            dk_more = lax.dot_general(
                grad_scores, query, (((0,), (0,)), ((), ())), preferred_element_type=jnp.float32
            )
            if index == last - 1:
                dv_total[:high] = dv_more
                dk_total[:high] = dk_more
            else:
                dv_total[:high] += dv_more
                dk_total[:high] += dk_more
        end = last * block
        dk_stage[inner, :end] = (dk_total[:end] * scale).astype(jnp.bfloat16)
        dv_stage[inner, :end] = dv_total[:end].astype(jnp.bfloat16)

    def key_sums(inner, label_row):
        key_float = k_all[inner].astype(jnp.float32)
        spread = jnp.mean(key_float * key_float, axis=1, keepdims=True)
        units = key_float * (lax.rsqrt(spread + 1e-06) * scale)
        units_high = units.astype(jnp.bfloat16)
        units_rest = (units - units_high.astype(jnp.float32)).astype(jnp.bfloat16)
        numbers = lax.broadcasted_iota(jnp.int32, (clusters, 1), 0)
        named = (numbers.astype(jnp.float32) == label_row).astype(jnp.bfloat16)
        owner_of = (numbers == slots_ref[rank * share + inner]).astype(jnp.bfloat16)
        chosen = jnp.dot(owner_of, named, preferred_element_type=jnp.float32).astype(jnp.bfloat16)
        sums_stage[inner] = jnp.dot(
            chosen, units_high, preferred_element_type=jnp.float32
        ) + jnp.dot(chosen, units_rest, preferred_element_type=jnp.float32)

    own_ids.wait()
    for step in range(1, owners):
        ids_in(fellow(0, step), me).wait_recv()

    for mine in range(parts):

        @pl.when(part == mine)
        def _():
            first, last = mine * owners // group, (mine + 1) * owners // group
            before = mine * owners
            for source in range(before):
                ids_in(source, me).wait_recv()
            for inner in range(share):
                labels = [
                    ids_all[index, inner].astype(jnp.float32) for index in range(before + owners)
                ]
                label_row = jnp.concatenate(labels, axis=1)
                label_columns = [
                    jnp.transpose(jnp.broadcast_to(label, (tokens, tokens)))[:, :1]
                    for label in labels
                ]
                for item in range(4):
                    own_in(item, inner).wait()
                    for step in range(1, owners):
                        head_in(item, inner, fellow(0, step), me).wait_recv()
                for item in range(2):
                    for source in range(before):
                        head_in(item, inner, source, me).wait_recv()
                attend(inner, first, last, label_row, label_columns)
                if inner == 0:
                    for away in range(1, parts - mine):
                        for step in range(owners):
                            for each in range(share):
                                for item in range(2):
                                    head_in(item, each, me, fellow(away, step)).wait_send()
                for target in range(before):
                    for item in range(2):
                        far_out(item, inner, me, target).start()
                for step in range(1, owners):
                    for item in range(4):
                        head_out(item, inner, me, fellow(0, step)).start()
                for item in range(4):
                    own_out(item, inner).start()
                if mine == parts - 1:
                    key_sums(inner, label_row)
                    for step in range(1, devices):
                        sums_out(inner, me, partner(step)).start()
                    own_sums(inner).start()
            for target in range(before):
                for inner in range(share):
                    for item in range(2):
                        far_out(item, inner, me, target).wait_send()
            for inner in range(share):
                if mine == parts - 1:
                    for step in range(1, devices):
                        sums_out(inner, me, partner(step)).wait_send()
                    own_sums(inner).wait()
                    for step in range(1, owners):
                        sums_out(inner, fellow(0, step), me).wait_recv()
                else:
                    for step in range(owners):
                        sums_out(inner, (parts - 1) * owners + step, me).wait_recv()

    for away in range(1, parts):

        @pl.when(part + away < parts)
        def _():
            for step in range(owners):
                ids_in(me, fellow(away, step)).wait_send()
                for inner in range(share):
                    for item in range(2):
                        far_out(item, inner, fellow(away, step), me).wait_recv()

    for step in range(1, owners):
        ids_in(me, fellow(0, step)).wait_send()
        for inner in range(share):
            for item in range(4):
                head_in(item, inner, me, fellow(0, step)).wait_send()
                head_out(item, inner, me, fellow(0, step)).wait_send()
                head_out(item, inner, fellow(0, step), me).wait_recv()
    for inner in range(share):
        for item in range(4):
            own_out(item, inner).wait()


def finish_kernel(
    help_size,
    owners,
    parts,
    att_ref,
    dq_ref,
    dk_ref,
    dv_ref,
    dk_far_ref,
    dv_far_ref,
    sums_ref,
    att_out,
    dq_out,
    dk_out,
    dv_out,
    sums_out,
):
    me = lax.axis_index("seq") * help_size + lax.axis_index("help")
    has_far = me // owners + 1 < parts
    att_out[...] = att_ref[...]
    dq_out[...] = dq_ref[...]
    sums_out[...] = sums_ref[...]
    for near, far, out in ((dk_ref, dk_far_ref, dk_out), (dv_ref, dv_far_ref, dv_out)):
        more = jnp.where(has_far, far[...].astype(jnp.float32), 0.0)
        out[...] = (near[...].astype(jnp.float32) + more).astype(out.dtype)


def routed_by_head(query_rows, key_rows, value_rows, out_grad, cluster_ids, cluster_slots):
    token_count, width = query_rows.shape
    local_heads, cluster_total = cluster_slots.shape
    depth = width // local_heads
    seq_size, help_size = lax.axis_size("seq"), lax.axis_size("help")
    devices = seq_size * help_size
    parts = 2
    owners = devices // parts
    if devices != local_heads or seq_size % parts or token_count != depth:
        return local(query_rows, key_rows, value_rows, out_grad, cluster_ids, cluster_slots)
    share = local_heads // owners
    total = devices * token_count
    low = jnp.bfloat16
    full = (share, total, depth)
    sums_shape = jax.ShapeDtypeStruct(
        (local_heads, cluster_total // devices, depth), jnp.float32
    )
    rows_shape = jax.ShapeDtypeStruct((token_count, width), low)
    landed = pl.pallas_call(
        functools.partial(head_kernel, seq_size, help_size, parts),
        out_shape=[rows_shape] * 6 + [sums_shape],
        in_specs=[pl.BlockSpec(memory_space=pltpu.HBM)] * 4
        + [pl.BlockSpec(memory_space=pltpu.VMEM)] * 2,
        out_specs=[pl.BlockSpec(memory_space=pl.ANY)] * 7,
        scratch_shapes=[pltpu.VMEM(full, low)] * 4
        + [pltpu.VMEM((devices, share, 1, token_count), jnp.int32)]
        + [pltpu.VMEM(full, low)] * 4
        + [pltpu.VMEM((share, cluster_total, depth), jnp.float32)]
        + [pltpu.VMEM((total, depth), jnp.float32)] * 2
        + [pltpu.SemaphoreType.DMA((share, devices, 4))] * 2
        + [pltpu.SemaphoreType.DMA((devices,))] * 2
        + [pltpu.SemaphoreType.DMA((share, devices, 4))] * 2
        + [pltpu.SemaphoreType.DMA((share, devices))] * 2,
        compiler_params=pltpu.CompilerParams(
            collective_id=0, has_side_effects=True, vmem_limit_bytes=60 * 1024 * 1024
        ),
    )(
        query_rows,
        key_rows,
        value_rows,
        out_grad,
        cluster_ids.reshape(local_heads, 1, token_count),
        cluster_slots.reshape(local_heads, 1, cluster_total),
    )
    return tuple(
        pl.pallas_call(
            functools.partial(finish_kernel, help_size, owners, parts),
            out_shape=[rows_shape] * 4 + [sums_shape],
            in_specs=[pl.BlockSpec(memory_space=pltpu.VMEM)] * 7,
            out_specs=[pl.BlockSpec(memory_space=pltpu.VMEM)] * 5,
            compiler_params=pltpu.CompilerParams(vmem_limit_bytes=60 * 1024 * 1024),
        )(*landed)
    )


def solution(mesh):
    in_specs = (
        P(("groups", "seq", "help"), "head"),
        P(("groups", "seq", "help"), "head"),
        P(("groups", "seq", "help"), "head"),
        P(("groups", "seq", "help"), "head"),
        P("head", ("groups", "seq", "help"), None),
        P(("groups", "head"), None),
    )
    out_specs = (
        P(("groups", "seq", "help"), "head"),
        P(("groups", "seq", "help"), "head"),
        P(("groups", "seq", "help"), "head"),
        P(("groups", "seq", "help"), "head"),
        P(("groups", "head"), ("seq", "help"), None),
    )
    return jax.shard_map(routed_by_head, mesh=mesh, in_specs=in_specs, out_specs=out_specs, check_vma=False)
```
